32 devices in a mesh: elem: 8 (over y, x, core), face: 4 (over z).
Axes of the slice: x: 2, y: 2, z: 4, core: 2. Of those that a mesh axis runs over, the one named last changes fastest.
Arguments:
- state: float32 [10, 72, 16384], P(None, None, ('elem', 'face')), may hold values from -6 to 6
- metric: float32 [16, 1024], P(None, ('elem', 'face')), may hold values from 0.5 to 2
- neighbours: int32 [4, 1024], P(None, ('elem', 'face')), may hold values from 0 to 1023, as said below
- cost_class: int32 [16, 1024], P(None, ('elem', 'face')), may hold values from 1 to 4
- batch_slot: int32 [16, 1024], replicated, may hold values from 0 to 16383, as said below
- level_mix: float32 [10, 72, 72], replicated, may hold values from -0.75 to 0.75
- field_coupling_matrix: float32 [10, 10], replicated, may hold values from -2 to 2
Outputs:
- state_out: float32 [10, 72, 16384], P(None, None, ('elem', 'face'))
- physics_state: float32 [10, 72, 16384], P(None, None, ('elem', 'face'))
The draws below stay inside these ranges and needn't reach their ends.
Inputs may be any that keep to these rules, and one draw needn't show every extreme that they name: Blocks are the element ranges [b * 32, (b + 1) * 32), in the order of the devices. The elements form a closed grid of rows of 8 elements, 4 rows a block; neighbours[0], [1], [2], [3] name the elements east, west, north and south, which are mutual (the west neighbour of the east one is the element itself, likewise north and south, and east of north is north of east). East and west neighbours lie in the element's own block; a north neighbour lies in the same block or in the next one, a south neighbour in the same block or the previous one, cyclically over the blocks; in each block exactly 8 elements have their north neighbour in the next block and 8 their south neighbour in the previous one. `batch_slot`: A permutation of the columns; batch c holds the places [c * 512, (c + 1) * 512). Every batch holds exactly 16 columns of every block, and within a batch cost_class never rises from one place to the next.
All inputs are finite; a program needn't handle non-finite values.
Results may differ from the reference program's by a relative error of at most 0.0001.
Values sent between devices are 32-bit elements; how exact they have to be, the bound alone decides.
A program may use at most 128 MiB of HBM per device.

```python
import math
import jax
import jax.numpy as jnp
import numpy as np
from jax import lax

F = 10
L = 72
NP2 = 16
ROWS_DEV = 4
SUBSTEPS = 3
SWEEPS = 4
E_DEV = 32
EW = 8
NELEM = 1024
NCOL = 16384


def invert_ids(permutation):
    extent = permutation.shape[0]
    return jnp.zeros((extent,), jnp.int32).at[permutation].set(jnp.arange(extent, dtype=jnp.int32))


def cost_classes_per_block(key):
    element_blocks = NELEM // E_DEV
    base = jax.random.fold_in(key, 23)
    storm_level = jax.random.randint(jax.random.fold_in(base, 1), (element_blocks,), 0, 4)
    quiet = jax.random.randint(jax.random.fold_in(base, 2), (element_blocks,), 0, 3)
    storm_level = jnp.where(quiet == 0, storm_level, 0)
    chosen = jax.random.randint(jax.random.fold_in(base, 3), (), 0, element_blocks)
    storm_level = jnp.where(jnp.arange(element_blocks) == chosen, 3, storm_level)
    raw_level = jax.random.randint(jax.random.fold_in(base, 4), (NP2, element_blocks, E_DEV), 0, 4)
    raw_level = raw_level.at[0, chosen, 0].set(3)
    return (1 + jnp.minimum(raw_level, storm_level[None, :, None])).astype(jnp.int32)


def draw_neighbours(key, part):
    element_blocks = NELEM // E_DEV
    block_keys = jax.random.split(jax.random.fold_in(key, 11), element_blocks)
    local_order = jax.vmap(lambda inner: jax.random.permutation(inner, E_DEV))(block_keys).astype(jnp.int32)
    slot_ids = local_order + (jnp.arange(element_blocks, dtype=jnp.int32) * E_DEV)[:, None]
    element_grid = slot_ids.reshape(element_blocks * ROWS_DEV, EW)
    east_ids = jnp.roll(element_grid, -1, axis=1)
    west_ids = jnp.roll(element_grid, 1, axis=1)
    north_ids = jnp.roll(element_grid, -1, axis=0)
    south_ids = jnp.roll(element_grid, 1, axis=0)
    neighbour_table = jnp.stack([east_ids, west_ids, north_ids, south_ids]).reshape(4, NELEM)
    flat_ids = element_grid.reshape(NELEM)
    return jnp.zeros((4, NELEM), jnp.int32).at[:, flat_ids].set(neighbour_table)


def draw_cost_class(key, part):
    return cost_classes_per_block(key).reshape(NP2, NELEM)


def draw_batch_slot(key, part):
    element_blocks = NELEM // E_DEV
    width = NP2 * E_DEV
    classes = cost_classes_per_block(key).transpose(1, 0, 2).reshape(element_blocks, width)
    base = jax.random.fold_in(key, 37)
    tie_keys = jax.random.split(jax.random.fold_in(base, 1), element_blocks)
    tie_break = jax.vmap(lambda inner: jax.random.permutation(inner, width))(tie_keys).astype(jnp.int32)
    score = (4 - classes) * width + tie_break
    sorted_order = jnp.argsort(score, axis=1)
    block_rank = jax.vmap(invert_ids)(sorted_order)
    rotation = jax.random.randint(jax.random.fold_in(base, 2), (element_blocks, 1), 0, element_blocks)
    destination = (block_rank + rotation) % element_blocks
    spread = jax.random.permutation(jax.random.fold_in(base, 3), element_blocks * width).astype(jnp.int32).reshape(element_blocks, width)
    global_key = (destination * 4 + (4 - classes)) * (element_blocks * width) + spread
    global_order = jnp.argsort(global_key.reshape(element_blocks * width))
    position = invert_ids(global_order)
    return position.reshape(element_blocks, NP2, E_DEV).transpose(1, 0, 2).reshape(NP2, NELEM)


def level_of(key, shape, pieces, low, top_value):
    loudness = 1.0
    for dim, blocks in pieces:
        steps = jax.random.uniform(jax.random.fold_in(jax.random.fold_in(key, 6), dim), (blocks,), jnp.float32, low / len(pieces), top_value / len(pieces))
        loudness = loudness * jnp.repeat(jnp.exp(steps), shape[dim] // blocks).reshape((-1,) + (1,) * (len(shape) - 1 - dim))
    return loudness


def normal_values(own_key, shape, deviation, limit, cuts=(), kind=jnp.bfloat16):
    loudness = level_of(own_key, shape, cuts, -0.22, 0.18) if cuts else 1.0
    entries = jax.random.normal(own_key, shape, jnp.float32) * deviation * loudness
    return jnp.minimum(jnp.maximum(entries, -limit), limit).astype(kind)


def setup_inputs(seed: int = 0) -> dict:
    keys = jax.random.split(jax.random.key(seed), 8)
    return {
        "state": normal_values(keys[0], (F, L, NCOL), 1.0, 6.0, ((2, 32),), jnp.float32),
        "metric": jnp.clip(jnp.exp(math.log(2.0) - 1.3862944 * jax.random.uniform(keys[1], (NP2, NELEM), jnp.float32) ** level_of(keys[1], (NP2, NELEM), ((1, 32),), -0.2, 0.2)), 0.5, 2.0),
        "neighbours": draw_neighbours(jax.random.fold_in(keys[7], 71), 0),
        "cost_class": draw_cost_class(jax.random.fold_in(keys[7], 71), 0),
        "batch_slot": draw_batch_slot(jax.random.fold_in(keys[7], 71), 0),
        "level_mix": normal_values(keys[5], (F, L, L), L ** -0.5, 0.75, (), jnp.float32),
        "field_coupling_matrix": normal_values(keys[6], (F, F), F ** -0.5, 2.0, (), jnp.float32),
    }


PHYSICS_RATE = 0.1
TIME_STEP = 0.02

def gll_matrices():
    gll_nodes = np.array([-1.0, -1.0 / np.sqrt(5.0), 1.0 / np.sqrt(5.0), 1.0])
    derivative = np.zeros((4, 4))
    for target in range(4):
        for source in range(4):
            if target == source:
                derivative[target, source] = sum((1.0 / (gll_nodes[source] - gll_nodes[middle]) for middle in range(4) if middle != source))
            else:
                numerator = np.prod([gll_nodes[target] - gll_nodes[middle] for middle in range(4) if middle != source and middle != target])
                denominator = np.prod([gll_nodes[source] - gll_nodes[middle] for middle in range(4) if middle != source])
                derivative[target, source] = numerator / denominator
    across = np.kron(np.eye(4), derivative).astype(np.float32)
    upward = np.kron(derivative, np.eye(4)).astype(np.float32)
    return (jnp.asarray(across), jnp.asarray(upward))

def advect(current, across, upward):
    along_x = jnp.einsum('pq,...qe->...pe', across, current, precision=lax.Precision.HIGHEST)
    along_y = jnp.einsum('pq,...qe->...pe', upward, current, precision=lax.Precision.HIGHEST)
    return -(current[0:1] * along_x + current[1:2] * along_y)

def combine(values, neighbours):
    leading = values.shape[:-2]
    members = values.shape[-1]
    layout = values.reshape(leading + (4, 4, members))
    west_edge = layout[..., :, 0, :]
    east_edge = layout[..., :, 3, :]
    new_east = east_edge + jnp.take(west_edge, neighbours[0], axis=-1)
    new_west = west_edge + jnp.take(east_edge, neighbours[1], axis=-1)
    stepped = jnp.stack([new_west, layout[..., :, 1, :], layout[..., :, 2, :], new_east], axis=-2)
    south_row = stepped[..., 0, :, :]
    north_row = stepped[..., 3, :, :]
    north_side = jnp.take(south_row, neighbours[2], axis=-1)
    south_side = jnp.take(north_row, neighbours[3], axis=-1)
    physics_output = jnp.stack([south_row + south_side, stepped[..., 1, :, :], stepped[..., 2, :, :], north_row + north_side], axis=-3)
    return physics_output.reshape(values.shape)

def relax(segment, active, level_mix, field_coupling_matrix):
    level_blended = jnp.einsum('flm,fmc->flc', level_mix, segment, precision=lax.Precision.HIGHEST)
    field_coupled = jnp.einsum('mx,xaq->maq', field_coupling_matrix, level_blended, precision=lax.Precision.HIGHEST)
    return jnp.where(active[None, None, :], segment + PHYSICS_RATE * jnp.tanh(field_coupled), segment)

def reference(state, metric, neighbours, cost_class, batch_slot, level_mix, field_coupling_matrix):
    fields, levels, total = state.shape
    points = metric.shape[0]
    members = metric.shape[1]
    grid_state = jnp.transpose(state.reshape(fields, levels, members, points), (0, 1, 3, 2))
    columns = grid_state.reshape(fields, levels, total)
    weighted = cost_class.reshape(total) * SWEEPS

    def physics_pass(threshold, advanced):
        return relax(advanced, weighted > threshold, level_mix, field_coupling_matrix)
    advanced = lax.fori_loop(0, 4 * SWEEPS, physics_pass, columns)
    physics_state = jnp.zeros_like(advanced).at[:, :, batch_slot.reshape(total)].set(advanced)
    physics_tendency = (advanced - columns).reshape(grid_state.shape)
    across, upward = gll_matrices()
    mass_total = combine(metric, neighbours)

    def per_level(bundle):
        current, change = bundle
        for advection_substep in range(SUBSTEPS):
            rate = advect(current, across, upward)
            updated = current + TIME_STEP * rate + change / SUBSTEPS
            current = combine(metric * updated, neighbours) / mass_total
        return current
    layered = lax.map(per_level, (jnp.moveaxis(grid_state, 1, 0), jnp.moveaxis(physics_tendency, 1, 0)))
    final = jnp.moveaxis(layered, 0, 1)
    state_out = jnp.transpose(final, (0, 1, 3, 2)).reshape(fields, levels, total)
    return (state_out, physics_state)
```

```python
from functools import partial

import jax
import jax.numpy as jnp
import numpy as np
from jax import lax
from jax.experimental import pallas as pl
from jax.experimental.pallas import tpu as pltpu
from jax.sharding import PartitionSpec as P

ROWS_DEV = 4
SUBSTEPS = 3
SWEEPS = 4
CLASSES = 4
PHYSICS_RATE = 0.1
TIME_STEP = 0.02
AXES = ("elem", "face")
EXTRA = 8
F32, BF16 = jnp.float32, jnp.bfloat16
VMEM_LIMIT = 56 * 1024 * 1024

EAST_WEST, NORTH_SOUTH, SEND_UP, SEND_DOWN, FROM_NEXT, FROM_PREV, BY_CLASS, BY_SLOT, SLOT, COST = range(10)
TABLE_ROWS = 16


def derivative_matrix():
    nodes = np.array([-1.0, -1.0 / np.sqrt(5.0), 1.0 / np.sqrt(5.0), 1.0])
    derivative = np.zeros((4, 4))
    for i in range(4):
        for j in range(4):
            if i == j:
                derivative[i, j] = sum(1.0 / (nodes[j] - nodes[m]) for m in range(4) if m != j)
            else:
                top = np.prod([nodes[i] - nodes[m] for m in range(4) if m not in (i, j)])
                derivative[i, j] = top / np.prod([nodes[j] - nodes[m] for m in range(4) if m != j])
    return derivative


def derivative_operators(width):
    derivative = derivative_matrix()
    blocks = np.eye(width // 16)
    across = np.kron(blocks, np.kron(np.eye(4), derivative)).T
    upward = np.kron(blocks, np.kron(derivative, np.eye(4))).T
    both = np.concatenate([across, upward], axis=1).astype(np.float32)
    high = both.astype(jnp.bfloat16)
    low = (both - high.astype(np.float32)).astype(jnp.bfloat16)
    return high, low


def split(values):
    high = values.astype(BF16)
    return high, (values - high.astype(F32)).astype(BF16)


def nn(a, b):
    return jnp.dot(a, b, preferred_element_type=F32)


def nt(a, b):
    return lax.dot_general(a, b, (((1,), (1,)), ((), ())), preferred_element_type=F32)


def tn(a, b):
    return lax.dot_general(a, b, (((0,), (0,)), ((), ())), preferred_element_type=F32)


def onehot(row, count):
    picks = lax.broadcasted_iota(jnp.int32, (count, row.shape[1]), 0)
    return jnp.where(picks == row, 1.0, 0.0).astype(F32)


def physics_kernel(
    trips, table, state, mix, coupling, tendency, outgoing, gather_sum, send_rows, whi, wlo, wide, work
):
    rows, cols = state.shape
    levels = mix.shape[0]
    half = cols // 2

    def index(i):
        return table[i : i + 1, :]

    own = lax.broadcasted_iota(jnp.int32, (1, cols), 1)
    identity = onehot(own, cols)
    first = (identity + onehot(index(EAST_WEST), cols)).astype(BF16)
    second = (identity + onehot(index(NORTH_SOUTH), cols)).astype(BF16)
    gather_sum[...] = nn(first, second).astype(BF16)
    edge = send_rows.shape[0] // 2
    chosen = jnp.concatenate([onehot(index(SEND_UP), edge), onehot(index(SEND_DOWN), edge)], axis=0)
    send_rows[...] = nt(chosen.astype(BF16), first).astype(BF16)

    for g in range(rows // levels):
        wide[g * levels : (g + 1) * levels, :] = mix[...] * coupling[g : g + 1, :]
    high, low = split(wide[...])
    whi[...] = high
    wlo[...] = low

    order = onehot(index(BY_CLASS), cols).astype(BF16)
    xh, xl = split(state[...])
    begin = nt(xh, order) + nt(xl, order)
    tendency[...] = begin
    work[...] = begin
    bound = index(COST) * SWEEPS

    def step(width, k, carry):
        x = work[:, :width]
        high, low = split(x)
        y = nn(whi[...], high) + nn(whi[...], low) + nn(wlo[...], high)
        work[:, :width] = jnp.where(bound[:, :width] > k, x + PHYSICS_RATE * jnp.tanh(y), x)
        return carry

    lax.fori_loop(0, trips[0], partial(step, cols), 0)
    lax.fori_loop(trips[0], trips[1], partial(step, half), 0)

    high, low = split(work[...] - tendency[...])
    change = nn(high, order) + nn(low, order)
    tendency[...] = change
    slots = jnp.broadcast_to(index(SLOT).astype(F32), (EXTRA, cols))
    high, low = split(jnp.concatenate([state[...] + change, slots], axis=0))
    to_slot = onehot(index(BY_SLOT), cols).astype(BF16)
    outgoing[...] = nt(to_slot, high) + nt(to_slot, low)


def move(current, tendency, metric, dhi, dlo, gather_sum, send_rows, levels):
    rows, cols = current.shape
    width = dhi.shape[0]
    parts = []
    for start in range(0, cols, width):
        x = current[:, start : start + width]
        high, low = split(x)
        slopes = nn(high, dhi) + nn(low, dhi) + nn(high, dlo)
        u, v = x[:levels], x[levels : 2 * levels]
        fields = rows // levels
        u, v = jnp.concatenate([u] * fields, axis=0), jnp.concatenate([v] * fields, axis=0)
        parts.append(u * slopes[:, :width] + v * slopes[:, width:])
    rate = -jnp.concatenate(parts, axis=1)
    moved = current + TIME_STEP * rate + tendency / SUBSTEPS
    weighted = jnp.concatenate([metric * moved, jnp.broadcast_to(metric, (EXTRA, cols))], axis=0)
    high, low = split(weighted)
    return nn(high, gather_sum) + nn(low, gather_sum), nt(send_rows, high) + nt(send_rows, low)


def settle(local, from_next, from_prev, table, rows):
    edge = from_next.shape[0]
    place_next = onehot(table[FROM_NEXT : FROM_NEXT + 1, :], edge)
    place_prev = onehot(table[FROM_PREV : FROM_PREV + 1, :], edge)
    place = jnp.concatenate([place_next, place_prev], axis=0).astype(BF16)
    high, low = split(jnp.concatenate([from_next, from_prev], axis=0))
    total = local + tn(high, place) + tn(low, place)
    return total[:rows] / total[rows : rows + 1]


def first_kernel(levels, state, tendency, metric, dhi, dlo, gather_sum, send_rows, local, up, down):
    edge = up.shape[0]
    total, rows = move(
        state[...], tendency[...], metric[...], dhi[...], dlo[...], gather_sum[...], send_rows[...], levels
    )
    local[...] = total
    up[...] = rows[:edge]
    down[...] = rows[edge:]


def middle_kernel(
    levels, before, from_next, from_prev, table, tendency, metric, dhi, dlo, gather_sum, send_rows, local, up, down
):
    edge = up.shape[0]
    current = settle(before[...], from_next[...], from_prev[...], table[...], tendency.shape[0])
    total, rows = move(
        current, tendency[...], metric[...], dhi[...], dlo[...], gather_sum[...], send_rows[...], levels
    )
    local[...] = total
    up[...] = rows[:edge]
    down[...] = rows[edge:]


def last_kernel(before, from_next, from_prev, table, out):
    out[...] = settle(before[...], from_next[...], from_prev[...], table[...], out.shape[0])


def place_kernel(arrived, out):
    rows, cols = out.shape
    slot = arrived[:, rows : rows + 1]
    places = lax.broadcasted_iota(jnp.int32, (cols, cols), 1).astype(F32)
    put = jnp.where(places == slot, 1.0, 0.0).astype(BF16)
    high, low = split(arrived[:, :rows])
    out[...] = tn(high, put) + tn(low, put)


def shifted(array, by):
    length = lax.axis_size(AXES)
    return lax.ppermute(array, AXES, [(i, (i + by) % length) for i in range(length)])


def per_column(row, points):
    return jnp.broadcast_to(row[:, None], (row.shape[0], points)).reshape(-1)


def rank(keys, valid=None):
    smaller = keys[None, :] < keys[:, None]
    if valid is not None:
        smaller &= valid[None, :]
    return jnp.sum(smaller.astype(jnp.int32), axis=1)


def index_table(neighbours, classes, slots, points, myself):
    members = neighbours.shape[1]
    cols = members * points
    base = myself * members
    point = jnp.arange(cols, dtype=jnp.int32) % points
    ix, iy = point % 4, point // 4
    sequence = jnp.arange(members, dtype=jnp.int32)
    remote_up = neighbours[2] // members != myself
    remote_down = neighbours[3] // members != myself
    wide = partial(per_column, points=points)
    east, west, north, south = (wide(neighbours[i] - base) for i in range(4))
    up, down = wide(remote_up), wide(remote_down)
    top, bottom = iy == 3, iy == 0
    east_west = jnp.where(
        ix == 3, points * east + 4 * iy, jnp.where(ix == 0, points * west + 4 * iy + 3, -1)
    )
    north_south = jnp.where(
        top & ~up, points * north + ix, jnp.where(bottom & ~down, points * south + 12 + ix, -1)
    )
    send_up = jnp.where(top & up, 4 * wide(rank(sequence, remote_up)) + ix, -1)
    send_down = jnp.where(bottom & down, 4 * wide(rank(sequence, remote_down)) + ix, -1)
    from_next = jnp.where(top & up, 4 * wide(rank(neighbours[2], remote_up)) + ix, -1)
    from_prev = jnp.where(bottom & down, 4 * wide(rank(neighbours[3], remote_down)) + ix, -1)
    own = jnp.arange(cols, dtype=jnp.int32)
    by_class = rank(own - classes * cols)
    by_slot = rank(slots)
    counts = [jnp.sum((classes >= q).astype(jnp.int32)) for q in range(1, CLASSES + 1)]
    cost = sum((count > own).astype(jnp.int32) for count in counts)
    some = sum((count > cols // 2).astype(jnp.int32) for count in counts)
    most = sum((count > 0).astype(jnp.int32) for count in counts)
    trips = jnp.stack([some, most]) * SWEEPS
    rows = [east_west, north_south, send_up, send_down, from_next, from_prev, by_class, by_slot, slots % cols, cost]
    rows += [jnp.zeros_like(own)] * (TABLE_ROWS - len(rows))
    return jnp.stack(rows), trips


def call(kernel, out_shape, scratch=(), smem=0, inputs=1):
    vmem = pl.BlockSpec(memory_space=pltpu.VMEM)
    return pl.pallas_call(
        kernel,
        out_shape=out_shape,
        in_specs=[pl.BlockSpec(memory_space=pltpu.SMEM)] * smem + [vmem] * (inputs - smem),
        out_specs=jax.tree.map(lambda _: vmem, out_shape),
        scratch_shapes=list(scratch),
        compiler_params=pltpu.CompilerParams(vmem_limit_bytes=VMEM_LIMIT),
    )


def per_device(state, metric, neighbours, cost_class, batch_slot, level_mix, field_coupling_matrix):
    fields, levels, cols = state.shape
    points, members = metric.shape
    rows = fields * levels
    edge = 4 * (members // ROWS_DEV)
    myself = lax.axis_index(AXES)
    slots = lax.dynamic_slice_in_dim(batch_slot, myself * members, members, axis=1).T.reshape(cols)
    table, trips = index_table(neighbours, cost_class.T.reshape(cols), slots, points, myself)
    flat = state.reshape(rows, cols)
    weight = metric.T.reshape(1, cols)
    mix = jnp.transpose(level_mix, (1, 0, 2)).reshape(levels, rows)
    coupling = jnp.broadcast_to(field_coupling_matrix[:, :, None], (fields, fields, levels)).reshape(fields, rows)
    dhi, dlo = (jnp.asarray(m) for m in derivative_operators(min(cols, 256)))

    shape = jax.ShapeDtypeStruct
    tendency, outgoing, gather_sum, send_rows = call(
        physics_kernel,
        (
            shape((rows, cols), F32),
            shape((cols, rows + EXTRA), F32),
            shape((cols, cols), BF16),
            shape((2 * edge, cols), BF16),
        ),
        (
            pltpu.VMEM((rows, rows), BF16),
            pltpu.VMEM((rows, rows), BF16),
            pltpu.VMEM((rows, rows), F32),
            pltpu.VMEM((rows, cols), F32),
        ),
        smem=1,
        inputs=5,
    )(trips, table, flat, mix, coupling)
    arrived = lax.all_to_all(outgoing, AXES, split_axis=0, concat_axis=0, tiled=True)

    partly = (
        shape((rows + EXTRA, cols), F32),
        shape((edge, rows + EXTRA), F32),
        shape((edge, rows + EXTRA), F32),
    )
    fixed = (tendency, weight, dhi, dlo, gather_sum, send_rows)
    local, up, down = call(partial(first_kernel, levels), partly, inputs=7)(flat, *fixed)
    for _ in range(SUBSTEPS - 1):
        from_prev, from_next = shifted(up, 1), shifted(down, -1)
        local, up, down = call(partial(middle_kernel, levels), partly, inputs=10)(
            local, from_next, from_prev, table, *fixed
        )
    from_prev, from_next = shifted(up, 1), shifted(down, -1)
    out = call(last_kernel, shape((rows, cols), F32), inputs=4)(local, from_next, from_prev, table)
    physics = call(place_kernel, shape((rows, cols), F32), inputs=1)(arrived)
    return out.reshape(state.shape), physics.reshape(state.shape)


def solution(mesh):
    split_cols = P(None, AXES)
    return jax.shard_map(
        per_device,
        mesh=mesh,
        in_specs=(P(None, None, AXES), split_cols, split_cols, split_cols, P(), P(), P()),
        out_specs=(P(None, None, AXES), P(None, None, AXES)),
        check_vma=False,
    )
```

```python
from functools import partial

import jax
import jax.numpy as jnp
import numpy as np
from jax import lax
from jax.experimental import pallas as pl
from jax.experimental.pallas import tpu as pltpu
from jax.sharding import PartitionSpec as P

ROWS_DEV = 4
SUBSTEPS = 3
SWEEPS = 4
CLASSES = 4
PHYSICS_RATE = 0.1
TIME_STEP = 0.02
AXES = ("elem", "face")
EXTRA = 8
F32, BF16 = jnp.float32, jnp.bfloat16
VMEM_LIMIT = 56 * 1024 * 1024

EAST_WEST, NORTH_SOUTH, SEND_UP, SEND_DOWN, FROM_NEXT, FROM_PREV, BY_CLASS, BY_SLOT, SLOT, COST = range(10)
TABLE_ROWS = 16


def derivative_matrix():
    nodes = np.array([-1.0, -1.0 / np.sqrt(5.0), 1.0 / np.sqrt(5.0), 1.0])
    derivative = np.zeros((4, 4))
    for i in range(4):
        for j in range(4):
            if i == j:
                derivative[i, j] = sum(1.0 / (nodes[j] - nodes[m]) for m in range(4) if m != j)
            else:
                top = np.prod([nodes[i] - nodes[m] for m in range(4) if m not in (i, j)])
                derivative[i, j] = top / np.prod([nodes[j] - nodes[m] for m in range(4) if m != j])
    return derivative


def derivative_operators(width):
    derivative = derivative_matrix()
    blocks = np.eye(width // 16)
    across = np.kron(blocks, np.kron(np.eye(4), derivative)).T
    upward = np.kron(blocks, np.kron(derivative, np.eye(4))).T
    both = np.concatenate([across, upward], axis=1).astype(np.float32)
    high = both.astype(jnp.bfloat16)
    low = (both - high.astype(np.float32)).astype(jnp.bfloat16)
    return high, low


def split(values):
    high = values.astype(BF16)
    return high, (values - high.astype(F32)).astype(BF16)


def nn(a, b):
    return jnp.dot(a, b, preferred_element_type=F32)


def nt(a, b):
    return lax.dot_general(a, b, (((1,), (1,)), ((), ())), preferred_element_type=F32)


def tn(a, b):
    return lax.dot_general(a, b, (((0,), (0,)), ((), ())), preferred_element_type=F32)


def onehot(row, count):
    picks = lax.broadcasted_iota(jnp.int32, (count, row.shape[1]), 0)
    return jnp.where(picks == row, 1.0, 0.0).astype(F32)


def physics_kernel(
    trips, table, state, mix, coupling, tendency, outgoing, gather_sum, send_rows, whi, wlo, wide, work
):
    rows, cols = state.shape
    levels = mix.shape[0]
    half = cols // 2

    def index(i):
        return table[i : i + 1, :]

    own = lax.broadcasted_iota(jnp.int32, (1, cols), 1)
    identity = onehot(own, cols)
    first = (identity + onehot(index(EAST_WEST), cols)).astype(BF16)
    second = (identity + onehot(index(NORTH_SOUTH), cols)).astype(BF16)
    gather_sum[...] = nn(first, second).astype(BF16)
    edge = send_rows.shape[0] // 2
    chosen = jnp.concatenate([onehot(index(SEND_UP), edge), onehot(index(SEND_DOWN), edge)], axis=0)
    send_rows[...] = nt(chosen.astype(BF16), first).astype(BF16)

    for g in range(rows // levels):
        wide[g * levels : (g + 1) * levels, :] = mix[...] * coupling[g : g + 1, :]
    high, low = split(wide[...])
    whi[...] = high
    wlo[...] = low

    order = onehot(index(BY_CLASS), cols).astype(BF16)
    xh, xl = split(state[...])
    begin = nt(xh, order) + nt(xl, order)
    tendency[...] = begin
    work[...] = begin
    bound = index(COST) * SWEEPS

    def step(width, k, carry):
        x = work[:, :width]
        high, low = split(x)
        y = nn(whi[...], high) + nn(whi[...], low) + nn(wlo[...], high)
        work[:, :width] = jnp.where(bound[:, :width] > k, x + PHYSICS_RATE * jnp.tanh(y), x)
        return carry

    lax.fori_loop(0, trips[0], partial(step, cols), 0)
    lax.fori_loop(trips[0], trips[1], partial(step, half), 0)

    high, low = split(work[...] - tendency[...])
    change = nn(high, order) + nn(low, order)
    tendency[...] = change
    slots = jnp.broadcast_to(index(SLOT).astype(F32), (EXTRA, cols))
    high, low = split(jnp.concatenate([state[...] + change, slots], axis=0))
    to_slot = onehot(index(BY_SLOT), outgoing.shape[0]).astype(BF16)
    outgoing[...] = nt(to_slot, high) + nt(to_slot, low)


def move(current, tendency, metric, dhi, dlo, gather_sum, send_rows, levels):
    rows, cols = current.shape
    width = dhi.shape[0]
    parts = []
    for start in range(0, cols, width):
        x = current[:, start : start + width]
        high, low = split(x)
        slopes = nn(high, dhi) + nn(low, dhi) + nn(high, dlo)
        u, v = x[:levels], x[levels : 2 * levels]
        fields = rows // levels
        u, v = jnp.concatenate([u] * fields, axis=0), jnp.concatenate([v] * fields, axis=0)
        parts.append(u * slopes[:, :width] + v * slopes[:, width:])
    rate = -jnp.concatenate(parts, axis=1)
    moved = current + TIME_STEP * rate + tendency / SUBSTEPS
    weighted = jnp.concatenate([metric * moved, jnp.broadcast_to(metric, (EXTRA, cols))], axis=0)
    high, low = split(weighted)
    return nn(high, gather_sum) + nn(low, gather_sum), nt(send_rows, high) + nt(send_rows, low)


def settle(local, from_next, from_prev, table, rows):
    edge = from_next.shape[0]
    place_next = onehot(table[FROM_NEXT : FROM_NEXT + 1, :], edge)
    place_prev = onehot(table[FROM_PREV : FROM_PREV + 1, :], edge)
    place = jnp.concatenate([place_next, place_prev], axis=0).astype(BF16)
    high, low = split(jnp.concatenate([from_next, from_prev], axis=0))
    total = local + tn(high, place) + tn(low, place)
    return total[:rows] / total[rows : rows + 1]


def exchange_kernel(
    levels, per, state, tendency, metric, dhi, dlo, gather_sum, send_rows, table, outgoing, out, physics,
    arrived, sent, received, near_send, near_recv, far_send, far_recv,
):
    rows, cols = out.shape
    edge = sent.shape[1] // 2
    elems, faces = lax.axis_size("elem"), lax.axis_size("face")
    devices = elems * faces
    myself = lax.axis_index("elem") * faces + lax.axis_index("face")

    def device(by):
        other = lax.rem(myself + by, devices)
        return other, (other // faces, lax.rem(other, faces))

    barrier = pltpu.get_barrier_semaphore()

    def greet(i, carry):
        pl.semaphore_signal(barrier, inc=1, device_id=device(i)[1], device_id_type=pl.DeviceIdType.MESH)
        return carry

    lax.fori_loop(1, devices, greet, 0)

    def near(step, way):
        return pltpu.make_async_remote_copy(
            src_ref=sent.at[step, pl.ds(way * edge, edge)],
            dst_ref=received.at[step, pl.ds((1 - way) * edge, edge)],
            send_sem=near_send.at[step, way],
            recv_sem=near_recv.at[step, way],
            device_id=device(1 if way == 0 else devices - 1)[1],
            device_id_type=pl.DeviceIdType.MESH,
        )

    def far(i):
        other, where = device(i)
        return pltpu.make_async_remote_copy(
            src_ref=outgoing.at[pl.ds(pl.multiple_of(other * per, 8), per)],
            dst_ref=arrived.at[pl.ds(pl.multiple_of(myself * per, 8), per)],
            send_sem=far_send.at[i],
            recv_sem=far_recv.at[i],
            device_id=where,
            device_id_type=pl.DeviceIdType.MESH,
        )

    def start_far(i, carry):
        far(i).start()
        return carry

    def wait_far(i, carry):
        far(i).wait()
        return carry

    def advance(current):
        return move(
            current, tendency[...], metric[...], dhi[...], dlo[...], gather_sum[...], send_rows[...], levels
        )

    local, edges = advance(state[...])
    sent[0] = edges
    pl.semaphore_wait(barrier, devices - 1)
    near(0, 0).start()
    near(0, 1).start()
    lax.fori_loop(1, devices, start_far, 0)
    mine = pl.ds(pl.multiple_of(myself * per, 8), per)
    arrived[mine, :] = outgoing[mine, :]
    for step in range(SUBSTEPS):
        near(step, 0).wait()
        near(step, 1).wait()
        current = settle(local, received[step, :edge], received[step, edge:], table[...], rows)
        if step < SUBSTEPS - 1:
            local, edges = advance(current)
            sent[step + 1] = edges
            near(step + 1, 0).start()
            near(step + 1, 1).start()
        else:
            out[...] = current
    lax.fori_loop(1, devices, wait_far, 0)
    slot = arrived[:, rows : rows + 1]
    places = lax.broadcasted_iota(jnp.int32, (arrived.shape[0], cols), 1).astype(F32)
    put = jnp.where(places == slot, 1.0, 0.0).astype(BF16)
    high, low = split(arrived[:, :rows])
    physics[...] = tn(high, put) + tn(low, put)


def per_column(row, points):
    return jnp.broadcast_to(row[:, None], (row.shape[0], points)).reshape(-1)


def rank(keys, valid=None):
    smaller = keys[None, :] < keys[:, None]
    if valid is not None:
        smaller &= valid[None, :]
    return jnp.sum(smaller.astype(jnp.int32), axis=1)


def index_table(neighbours, classes, slots, points, myself, per):
    members = neighbours.shape[1]
    cols = members * points
    base = myself * members
    point = jnp.arange(cols, dtype=jnp.int32) % points
    ix, iy = point % 4, point // 4
    sequence = jnp.arange(members, dtype=jnp.int32)
    remote_up = neighbours[2] // members != myself
    remote_down = neighbours[3] // members != myself
    wide = partial(per_column, points=points)
    east, west, north, south = (wide(neighbours[i] - base) for i in range(4))
    up, down = wide(remote_up), wide(remote_down)
    top, bottom = iy == 3, iy == 0
    east_west = jnp.where(
        ix == 3, points * east + 4 * iy, jnp.where(ix == 0, points * west + 4 * iy + 3, -1)
    )
    north_south = jnp.where(
        top & ~up, points * north + ix, jnp.where(bottom & ~down, points * south + 12 + ix, -1)
    )
    send_up = jnp.where(top & up, 4 * wide(rank(sequence, remote_up)) + ix, -1)
    send_down = jnp.where(bottom & down, 4 * wide(rank(sequence, remote_down)) + ix, -1)
    from_next = jnp.where(top & up, 4 * wide(rank(neighbours[2], remote_up)) + ix, -1)
    from_prev = jnp.where(bottom & down, 4 * wide(rank(neighbours[3], remote_down)) + ix, -1)
    own = jnp.arange(cols, dtype=jnp.int32)
    by_class = rank(own - classes * cols)
    by_slot = rank(slots)
    pair = cols // lax.axis_size(AXES)
    by_slot = by_slot // pair * per + by_slot % pair
    counts = [jnp.sum((classes >= q).astype(jnp.int32)) for q in range(1, CLASSES + 1)]
    cost = sum((count > own).astype(jnp.int32) for count in counts)
    some = sum((count > cols // 2).astype(jnp.int32) for count in counts)
    most = sum((count > 0).astype(jnp.int32) for count in counts)
    trips = jnp.stack([some, most]) * SWEEPS
    rows = [east_west, north_south, send_up, send_down, from_next, from_prev, by_class, by_slot, slots % cols, cost]
    rows += [jnp.zeros_like(own)] * (TABLE_ROWS - len(rows))
    return jnp.stack(rows), trips


def call(kernel, out_shape, scratch=(), smem=0, inputs=1, **params):
    vmem = pl.BlockSpec(memory_space=pltpu.VMEM)
    return pl.pallas_call(
        kernel,
        out_shape=out_shape,
        in_specs=[pl.BlockSpec(memory_space=pltpu.SMEM)] * smem + [vmem] * (inputs - smem),
        out_specs=jax.tree.map(lambda _: vmem, out_shape),
        scratch_shapes=list(scratch),
        compiler_params=pltpu.CompilerParams(vmem_limit_bytes=VMEM_LIMIT, **params),
    )


def per_device(state, metric, neighbours, cost_class, batch_slot, level_mix, field_coupling_matrix):
    fields, levels, cols = state.shape
    points, members = metric.shape
    rows = fields * levels
    edge = 4 * (members // ROWS_DEV)
    myself = lax.axis_index(AXES)
    devices = lax.axis_size(AXES)
    per = -(-(cols // devices) // 8) * 8
    slots = lax.dynamic_slice_in_dim(batch_slot, myself * members, members, axis=1).T.reshape(cols)
    table, trips = index_table(neighbours, cost_class.T.reshape(cols), slots, points, myself, per)
    flat = state.reshape(rows, cols)
    weight = metric.T.reshape(1, cols)
    mix = jnp.transpose(level_mix, (1, 0, 2)).reshape(levels, rows)
    coupling = jnp.broadcast_to(field_coupling_matrix[:, :, None], (fields, fields, levels)).reshape(fields, rows)
    dhi, dlo = (jnp.asarray(m) for m in derivative_operators(min(cols, 256)))

    shape = jax.ShapeDtypeStruct
    tendency, outgoing, gather_sum, send_rows = call(
        physics_kernel,
        (
            shape((rows, cols), F32),
            shape((devices * per, rows + EXTRA), F32),
            shape((cols, cols), BF16),
            shape((2 * edge, cols), BF16),
        ),
        (
            pltpu.VMEM((rows, rows), BF16),
            pltpu.VMEM((rows, rows), BF16),
            pltpu.VMEM((rows, rows), F32),
            pltpu.VMEM((rows, cols), F32),
        ),
        smem=1,
        inputs=5,
    )(trips, table, flat, mix, coupling)
    out, physics = call(
        partial(exchange_kernel, levels, per),
        (shape((rows, cols), F32), shape((rows, cols), F32)),
        (
            pltpu.VMEM((devices * per, rows + EXTRA), F32),
            pltpu.VMEM((SUBSTEPS, 2 * edge, rows + EXTRA), F32),
            pltpu.VMEM((SUBSTEPS, 2 * edge, rows + EXTRA), F32),
            pltpu.SemaphoreType.DMA((SUBSTEPS, 2)),
            pltpu.SemaphoreType.DMA((SUBSTEPS, 2)),
            pltpu.SemaphoreType.DMA((devices,)),
            pltpu.SemaphoreType.DMA((devices,)),
        ),
        inputs=9,
        collective_id=0,
        has_side_effects=True,
    )(flat, tendency, weight, dhi, dlo, gather_sum, send_rows, table, outgoing)
    return out.reshape(state.shape), physics.reshape(state.shape)


def solution(mesh):
    split_cols = P(None, AXES)
    return jax.shard_map(
        per_device,
        mesh=mesh,
        in_specs=(P(None, None, AXES), split_cols, split_cols, split_cols, P(), P(), P()),
        out_specs=(P(None, None, AXES), P(None, None, AXES)),
        check_vma=False,
    )
```

```python
from functools import partial

import jax
import jax.numpy as jnp
import numpy as np
from jax import lax
from jax.experimental import pallas as pl
from jax.experimental.pallas import tpu as pltpu
from jax.sharding import PartitionSpec as P

ROWS_DEV = 4
SUBSTEPS = 3
SWEEPS = 4
CLASSES = 4
PHYSICS_RATE = 0.1
TIME_STEP = 0.02
AXES = ("elem", "face")
EXTRA = 8
F32, BF16 = jnp.float32, jnp.bfloat16
VMEM_LIMIT = 56 * 1024 * 1024

FROM_NEXT, FROM_PREV, WEIGHT = range(3)
TABLE_ROWS = 8
FAR_AWAY = float(2**24)


def derivative_matrix():
    nodes = np.array([-1.0, -1.0 / np.sqrt(5.0), 1.0 / np.sqrt(5.0), 1.0])
    derivative = np.zeros((4, 4))
    for i in range(4):
        for j in range(4):
            if i == j:
                derivative[i, j] = sum(1.0 / (nodes[j] - nodes[m]) for m in range(4) if m != j)
            else:
                top = np.prod([nodes[i] - nodes[m] for m in range(4) if m not in (i, j)])
                derivative[i, j] = top / np.prod([nodes[j] - nodes[m] for m in range(4) if m != j])
    return derivative


def derivative_operators(width):
    derivative = derivative_matrix()
    blocks = np.eye(width // 16)
    across = np.kron(blocks, np.kron(np.eye(4), derivative)).T
    upward = np.kron(blocks, np.kron(derivative, np.eye(4))).T
    both = np.concatenate([across, upward], axis=1).astype(np.float32)
    high = both.astype(jnp.bfloat16)
    low = (both - high.astype(np.float32)).astype(jnp.bfloat16)
    return high, low


def split(values):
    high = values.astype(BF16)
    return high, (values - high.astype(F32)).astype(BF16)


def nn(a, b):
    return jnp.dot(a, b, preferred_element_type=F32)


def nt(a, b):
    return lax.dot_general(a, b, (((1,), (1,)), ((), ())), preferred_element_type=F32)


def tn(a, b):
    return lax.dot_general(a, b, (((0,), (0,)), ((), ())), preferred_element_type=F32)


def onehot(row, count):
    picks = lax.broadcasted_iota(jnp.int32, (count, row.shape[1]), 0).astype(F32)
    return jnp.where(picks == row, 1.0, 0.0).astype(F32)


def exact(a, b):
    return jnp.dot(a, b, precision=lax.Precision.HIGHEST, preferred_element_type=F32)


def index_rows(metric, neighbours, classes, slots):
    points, members = metric.shape
    cols = points * members
    base = ((lax.axis_index("elem") * lax.axis_size("face") + lax.axis_index("face")) * members).astype(F32)
    shift = points.bit_length() - 1
    own = lax.broadcasted_iota(jnp.int32, (1, cols), 1)
    element, point = (own >> shift).astype(F32), own & (points - 1)
    ix, iy = (point & 3).astype(F32), (point >> 2).astype(F32)
    leading = point == 0
    sequence = own.astype(F32)
    stacked = jnp.concatenate([metric, classes.astype(F32), slots.astype(F32)], axis=0)
    spread = onehot(element, members)
    rows = exact(stacked, spread)
    mine = lax.broadcasted_iota(jnp.int32, (points, cols), 0) == point
    weight, cost, slot = (
        jnp.sum(jnp.where(mine, rows[i * points : (i + 1) * points], 0.0), axis=0, keepdims=True) for i in range(3)
    )
    near = exact(neighbours.astype(F32), spread) - base
    east, west, north, south = (near[i : i + 1] for i in range(4))
    up = (north < 0.0) | (north >= members)
    down = (south < 0.0) | (south >= members)
    top, bottom = iy == 3.0, iy == 0.0

    keys = jnp.concatenate(
        [
            sequence - cost * cols,
            slot,
            jnp.where(up & leading, element, FAR_AWAY),
            jnp.where(down & leading, element, FAR_AWAY),
            jnp.where(up & leading, north, FAR_AWAY),
            jnp.where(down & leading, south, FAR_AWAY),
            sequence,
            sequence,
        ],
        axis=0,
    )
    turned = jnp.transpose(keys)

    def rank(i, values):
        return jnp.sum(jnp.where(turned[:, i : i + 1] < values, 1.0, 0.0), axis=0, keepdims=True)

    east_west = jnp.where(
        ix == 3.0, points * east + 4.0 * iy, jnp.where(ix == 0.0, points * west + 4.0 * iy + 3.0, -1.0)
    )
    north_south = jnp.where(
        top & ~up, points * north + ix, jnp.where(bottom & ~down, points * south + 12.0 + ix, -1.0)
    )
    send_up = jnp.where(top & up, 4.0 * rank(2, element) + ix, -1.0)
    send_down = jnp.where(bottom & down, 4.0 * rank(3, element) + ix, -1.0)
    from_next = jnp.where(top & up, 4.0 * rank(4, north) + ix, -1.0)
    from_prev = jnp.where(bottom & down, 4.0 * rank(5, south) + ix, -1.0)
    ordered = jnp.zeros((1, cols), F32)
    for q in range(1, CLASSES + 1):
        count = jnp.sum(jnp.where(cost >= q, 1.0, 0.0), axis=1, keepdims=True)
        ordered += jnp.where(sequence < count, 1.0, 0.0)
    return {
        "east_west": east_west,
        "north_south": north_south,
        "send_up": send_up,
        "send_down": send_down,
        "from_next": from_next,
        "from_prev": from_prev,
        "by_class": rank(0, keys[0:1]),
        "by_slot": rank(1, slot),
        "slot": slot,
        "weight": weight,
        "bound": ordered * SWEEPS,
    }


def physics_kernel(
    per, state, metric, neighbours, classes, slots, mix, coupling,
    tendency, outgoing, gather_sum, send_rows, table, whi, wlo, wide, work, spreadmix,
):
    rows, cols = state.shape
    fields, levels, _ = mix.shape
    half = cols // 2
    index = index_rows(metric[...], neighbours[...], classes[...], slots[...])
    blank = jnp.zeros((TABLE_ROWS - 3, cols), F32)
    table[...] = jnp.concatenate([index["from_next"], index["from_prev"], index["weight"], blank], axis=0)

    own = lax.broadcasted_iota(jnp.int32, (1, cols), 1).astype(F32)
    identity = onehot(own, cols)
    first = (identity + onehot(index["east_west"], cols)).astype(BF16)
    second = (identity + onehot(index["north_south"], cols)).astype(BF16)
    gather_sum[...] = nn(first, second).astype(BF16)
    edge = send_rows.shape[0] // 2
    chosen = jnp.concatenate([onehot(index["send_up"], edge), onehot(index["send_down"], edge)], axis=0)
    send_rows[...] = nt(chosen.astype(BF16), first).astype(BF16)

    place = lax.broadcasted_iota(jnp.int32, (fields, rows), 1)
    field = lax.broadcasted_iota(jnp.int32, (fields, rows), 0)
    inside = (place >= field * levels) & (place < (field + 1) * levels)
    gains = exact(coupling[...], jnp.where(inside, 1.0, 0.0))
    for f in range(fields):
        spreadmix[:, f * levels : (f + 1) * levels] = mix[f]
    for g in range(fields):
        wide[g * levels : (g + 1) * levels, :] = spreadmix[...] * gains[g : g + 1, :]
    high, low = split(wide[...])
    whi[...] = high
    wlo[...] = low

    order = onehot(index["by_class"], cols).astype(BF16)
    xh, xl = split(state[...])
    begin = nt(xh, order) + nt(xl, order)
    tendency[...] = begin
    work[...] = begin
    bound = index["bound"]
    later = jnp.where(own >= half, bound, 0.0)
    most, some = jnp.max(bound).astype(jnp.int32), jnp.max(later).astype(jnp.int32)

    def step(width, k, carry):
        x = work[:, :width]
        high, low = split(x)
        y = nn(whi[...], high) + nn(whi[...], low) + nn(wlo[...], high)
        work[:, :width] = jnp.where(bound[:, :width] > k.astype(F32), x + PHYSICS_RATE * jnp.tanh(y), x)
        return carry

    lax.fori_loop(0, some, partial(step, cols), 0)
    lax.fori_loop(some, most, partial(step, half), 0)

    high, low = split(work[...] - tendency[...])
    change = nn(high, order) + nn(low, order)
    tendency[...] = change
    slots = jnp.broadcast_to(index["slot"], (EXTRA, cols))
    high, low = split(jnp.concatenate([state[...] + change, slots], axis=0))
    spot = index["by_slot"]
    pair = cols // (outgoing.shape[0] // per)
    if pair != per:
        whole = spot.astype(jnp.int32)
        spot = (lax.div(whole, pair) * per + lax.rem(whole, pair)).astype(F32)
    to_slot = onehot(spot, outgoing.shape[0]).astype(BF16)
    outgoing[...] = nt(to_slot, high) + nt(to_slot, low)


def move(current, tendency, metric, dhi, dlo, gather_sum, send_rows, levels):
    rows, cols = current.shape
    width = dhi.shape[0]
    parts = []
    for start in range(0, cols, width):
        x = current[:, start : start + width]
        high, low = split(x)
        slopes = nn(high, dhi) + nn(low, dhi) + nn(high, dlo)
        u, v = x[:levels], x[levels : 2 * levels]
        fields = rows // levels
        u, v = jnp.concatenate([u] * fields, axis=0), jnp.concatenate([v] * fields, axis=0)
        parts.append(u * slopes[:, :width] + v * slopes[:, width:])
    rate = -jnp.concatenate(parts, axis=1)
    moved = current + TIME_STEP * rate + tendency / SUBSTEPS
    weighted = jnp.concatenate([metric * moved, jnp.broadcast_to(metric, (EXTRA, cols))], axis=0)
    high, low = split(weighted)
    return nn(high, gather_sum) + nn(low, gather_sum), nt(send_rows, high) + nt(send_rows, low)


def settle(local, from_next, from_prev, table, rows):
    edge = from_next.shape[0]
    place_next = onehot(table[FROM_NEXT : FROM_NEXT + 1, :], edge)
    place_prev = onehot(table[FROM_PREV : FROM_PREV + 1, :], edge)
    place = jnp.concatenate([place_next, place_prev], axis=0).astype(BF16)
    high, low = split(jnp.concatenate([from_next, from_prev], axis=0))
    total = local + tn(high, place) + tn(low, place)
    return total[:rows] / total[rows : rows + 1]


def exchange_kernel(
    levels, per, state, tendency, dhi, dlo, gather_sum, send_rows, table, outgoing, out, physics,
    arrived, sent, received, near_send, near_recv, far_send, far_recv,
):
    rows, cols = out.shape
    edge = sent.shape[1] // 2
    elems, faces = lax.axis_size("elem"), lax.axis_size("face")
    devices = elems * faces
    myself = lax.axis_index("elem") * faces + lax.axis_index("face")

    def device(by):
        other = lax.rem(myself + by, devices)
        return other, (other // faces, lax.rem(other, faces))

    barrier = pltpu.get_barrier_semaphore()

    def greet(i, carry):
        pl.semaphore_signal(barrier, inc=1, device_id=device(i)[1], device_id_type=pl.DeviceIdType.MESH)
        return carry

    lax.fori_loop(1, devices, greet, 0)

    def near(step, way):
        return pltpu.make_async_remote_copy(
            src_ref=sent.at[step, pl.ds(way * edge, edge)],
            dst_ref=received.at[step, pl.ds((1 - way) * edge, edge)],
            send_sem=near_send.at[step, way],
            recv_sem=near_recv.at[step, way],
            device_id=device(1 if way == 0 else devices - 1)[1],
            device_id_type=pl.DeviceIdType.MESH,
        )

    def far(i):
        other, where = device(i)
        return pltpu.make_async_remote_copy(
            src_ref=outgoing.at[pl.ds(pl.multiple_of(other * per, 8), per)],
            dst_ref=arrived.at[pl.ds(pl.multiple_of(myself * per, 8), per)],
            send_sem=far_send.at[i],
            recv_sem=far_recv.at[i],
            device_id=where,
            device_id_type=pl.DeviceIdType.MESH,
        )

    def start_far(i, carry):
        far(i).start()
        return carry

    def wait_far(i, carry):
        far(i).wait()
        return carry

    def advance(current):
        return move(
            current, tendency[...], table[WEIGHT : WEIGHT + 1, :], dhi[...], dlo[...], gather_sum[...], send_rows[...], levels
        )

    local, edges = advance(state[...])
    sent[0] = edges
    pl.semaphore_wait(barrier, devices - 1)
    near(0, 0).start()
    near(0, 1).start()
    cuts = [1, 1 + (devices - 1) // 4, 1 + (devices - 1) // 2, devices]
    lax.fori_loop(cuts[0], cuts[1], start_far, 0)
    mine = pl.ds(pl.multiple_of(myself * per, 8), per)
    arrived[mine, :] = outgoing[mine, :]
    for step in range(SUBSTEPS):
        near(step, 0).wait()
        near(step, 1).wait()
        current = settle(local, received[step, :edge], received[step, edge:], table[...], rows)
        if step < SUBSTEPS - 1:
            local, edges = advance(current)
            sent[step + 1] = edges
            near(step + 1, 0).start()
            near(step + 1, 1).start()
            lax.fori_loop(cuts[step + 1], cuts[step + 2], start_far, 0)
        else:
            out[...] = current
    lax.fori_loop(1, devices, wait_far, 0)
    slot = arrived[:, rows : rows + 1]
    places = lax.broadcasted_iota(jnp.int32, (arrived.shape[0], cols), 1).astype(F32)
    put = jnp.where(places == slot - (myself * cols).astype(F32), 1.0, 0.0).astype(BF16)
    high, low = split(arrived[:, :rows])
    physics[...] = tn(high, put) + tn(low, put)


def call(kernel, out_shape, scratch=(), inputs=1, **params):
    vmem = pl.BlockSpec(memory_space=pltpu.VMEM)
    return pl.pallas_call(
        kernel,
        out_shape=out_shape,
        in_specs=[vmem] * inputs,
        out_specs=jax.tree.map(lambda _: vmem, out_shape),
        scratch_shapes=list(scratch),
        compiler_params=pltpu.CompilerParams(vmem_limit_bytes=VMEM_LIMIT, **params),
    )


def per_device(state, metric, neighbours, cost_class, batch_slot, level_mix, field_coupling_matrix):
    fields, levels, cols = state.shape
    points, members = metric.shape
    rows = fields * levels
    edge = 4 * (members // ROWS_DEV)
    myself = lax.axis_index(AXES)
    devices = lax.axis_size(AXES)
    per = -(-(cols // devices) // 8) * 8
    slots = lax.dynamic_slice_in_dim(batch_slot, myself * members, members, axis=1)
    flat = state.reshape(rows, cols)
    dhi, dlo = (jnp.asarray(m) for m in derivative_operators(min(cols, 256)))

    shape = jax.ShapeDtypeStruct
    tendency, outgoing, gather_sum, send_rows, table = call(
        partial(physics_kernel, per),
        (
            shape((rows, cols), F32),
            shape((devices * per, rows + EXTRA), F32),
            shape((cols, cols), BF16),
            shape((2 * edge, cols), BF16),
            shape((TABLE_ROWS, cols), F32),
        ),
        (
            pltpu.VMEM((rows, rows), BF16),
            pltpu.VMEM((rows, rows), BF16),
            pltpu.VMEM((rows, rows), F32),
            pltpu.VMEM((rows, cols), F32),
            pltpu.VMEM((levels, rows), F32),
        ),
        inputs=7,
    )(flat, metric, neighbours, cost_class, slots, level_mix, field_coupling_matrix)
    out, physics = call(
        partial(exchange_kernel, levels, per),
        (shape((rows, cols), F32), shape((rows, cols), F32)),
        (
            pltpu.VMEM((devices * per, rows + EXTRA), F32),
            pltpu.VMEM((SUBSTEPS, 2 * edge, rows + EXTRA), F32),
            pltpu.VMEM((SUBSTEPS, 2 * edge, rows + EXTRA), F32),
            pltpu.SemaphoreType.DMA((SUBSTEPS, 2)),
            pltpu.SemaphoreType.DMA((SUBSTEPS, 2)),
            pltpu.SemaphoreType.DMA((devices,)),
            pltpu.SemaphoreType.DMA((devices,)),
        ),
        inputs=8,
        collective_id=0,
        has_side_effects=True,
    )(flat, tendency, dhi, dlo, gather_sum, send_rows, table, outgoing)
    return out.reshape(state.shape), physics.reshape(state.shape)


def solution(mesh):
    split_cols = P(None, AXES)
    return jax.shard_map(
        per_device,
        mesh=mesh,
        in_specs=(P(None, None, AXES), split_cols, split_cols, split_cols, P(), P(), P()),
        out_specs=(P(None, None, AXES), P(None, None, AXES)),
        check_vma=False,
    )
```

```python
import math
from functools import partial

import jax
import jax.numpy as jnp
import numpy as np
from jax import lax
from jax.experimental import pallas as pl
from jax.experimental.pallas import tpu as pltpu
from jax.sharding import PartitionSpec as P

ROWS_DEV = 4
SUBSTEPS = 3
SWEEPS = 4
CLASSES = 4
PHYSICS_RATE = 0.1
TIME_STEP = 0.02
AXES = ("elem", "face")
EXTRA = 8
F32, BF16 = jnp.float32, jnp.bfloat16
VMEM_LIMIT = 56 * 1024 * 1024

FROM_NEXT, FROM_PREV, WEIGHT = range(3)
TABLE_ROWS = 8
FAR_AWAY = float(2**24)


def derivative_matrix():
    nodes = np.array([-1.0, -1.0 / np.sqrt(5.0), 1.0 / np.sqrt(5.0), 1.0])
    derivative = np.zeros((4, 4))
    for i in range(4):
        for j in range(4):
            if i == j:
                derivative[i, j] = sum(1.0 / (nodes[j] - nodes[m]) for m in range(4) if m != j)
            else:
                top = np.prod([nodes[i] - nodes[m] for m in range(4) if m not in (i, j)])
                derivative[i, j] = top / np.prod([nodes[j] - nodes[m] for m in range(4) if m != j])
    return derivative


def derivative_operators(width):
    derivative = derivative_matrix()
    blocks = np.eye(width // 16)
    across = np.kron(blocks, np.kron(np.eye(4), derivative)).T
    upward = np.kron(blocks, np.kron(derivative, np.eye(4))).T
    both = np.concatenate([across, upward], axis=1).astype(np.float32)
    high = both.astype(jnp.bfloat16)
    low = (both - high.astype(np.float32)).astype(jnp.bfloat16)
    return high, low


def split(values):
    high = values.astype(BF16)
    return high, (values - high.astype(F32)).astype(BF16)


def nn(a, b):
    return jnp.dot(a, b, preferred_element_type=F32)


def nt(a, b):
    return lax.dot_general(a, b, (((1,), (1,)), ((), ())), preferred_element_type=F32)


def tn(a, b):
    return lax.dot_general(a, b, (((0,), (0,)), ((), ())), preferred_element_type=F32)


def onehot(row, count):
    picks = lax.broadcasted_iota(jnp.int32, (count, row.shape[1]), 0).astype(F32)
    return jnp.where(picks == row, 1.0, 0.0).astype(F32)


def exact(a, b):
    return jnp.dot(a, b, precision=lax.Precision.HIGHEST, preferred_element_type=F32)


def index_rows(metric, neighbours, classes, slots):
    points, members = metric.shape
    cols = points * members
    base = ((lax.axis_index("elem") * lax.axis_size("face") + lax.axis_index("face")) * members).astype(F32)
    shift = points.bit_length() - 1
    own = lax.broadcasted_iota(jnp.int32, (1, cols), 1)
    element, point = (own >> shift).astype(F32), own & (points - 1)
    ix, iy = (point & 3).astype(F32), (point >> 2).astype(F32)
    leading = point == 0
    sequence = own.astype(F32)
    stacked = jnp.concatenate([metric, classes.astype(F32), slots.astype(F32)], axis=0)
    spread = onehot(element, members)
    rows = exact(stacked, spread)
    mine = lax.broadcasted_iota(jnp.int32, (points, cols), 0) == point
    weight, cost, slot = (
        jnp.sum(jnp.where(mine, rows[i * points : (i + 1) * points], 0.0), axis=0, keepdims=True) for i in range(3)
    )
    near = exact(neighbours.astype(F32), spread) - base
    east, west, north, south = (near[i : i + 1] for i in range(4))
    up = (north < 0.0) | (north >= members)
    down = (south < 0.0) | (south >= members)
    top, bottom = iy == 3.0, iy == 0.0

    keys = jnp.concatenate(
        [
            sequence - cost * cols,
            slot,
            jnp.where(up & leading, element, FAR_AWAY),
            jnp.where(down & leading, element, FAR_AWAY),
            jnp.where(up & leading, north, FAR_AWAY),
            jnp.where(down & leading, south, FAR_AWAY),
            sequence,
            sequence,
        ],
        axis=0,
    )
    turned = jnp.transpose(keys)

    def rank(i, values):
        return jnp.sum(jnp.where(turned[:, i : i + 1] < values, 1.0, 0.0), axis=0, keepdims=True)

    east_west = jnp.where(
        ix == 3.0, points * east + 4.0 * iy, jnp.where(ix == 0.0, points * west + 4.0 * iy + 3.0, -1.0)
    )
    north_south = jnp.where(
        top & ~up, points * north + ix, jnp.where(bottom & ~down, points * south + 12.0 + ix, -1.0)
    )
    send_up = jnp.where(top & up, 4.0 * rank(2, element) + ix, -1.0)
    send_down = jnp.where(bottom & down, 4.0 * rank(3, element) + ix, -1.0)
    from_next = jnp.where(top & up, 4.0 * rank(4, north) + ix, -1.0)
    from_prev = jnp.where(bottom & down, 4.0 * rank(5, south) + ix, -1.0)
    ordered = jnp.zeros((1, cols), F32)
    for q in range(1, CLASSES + 1):
        count = jnp.sum(jnp.where(cost >= q, 1.0, 0.0), axis=1, keepdims=True)
        ordered += jnp.where(sequence < count, 1.0, 0.0)
    return {
        "east_west": east_west,
        "north_south": north_south,
        "send_up": send_up,
        "send_down": send_down,
        "from_next": from_next,
        "from_prev": from_prev,
        "by_class": rank(0, keys[0:1]),
        "by_slot": rank(1, slot),
        "slot": slot,
        "weight": weight,
        "bound": ordered * SWEEPS,
    }


def physics_kernel(
    per, state, metric, neighbours, classes, slots, mix, coupling,
    tendency, outgoing, gather_sum, send_rows, table, whi, wlo, wide, work, spreadmix,
):
    rows, cols = state.shape
    fields, levels, _ = mix.shape
    half = cols // 2
    index = index_rows(metric[...], neighbours[...], classes[...], slots[...])
    blank = jnp.zeros((TABLE_ROWS - 3, cols), F32)
    table[...] = jnp.concatenate([index["from_next"], index["from_prev"], index["weight"], blank], axis=0)

    own = lax.broadcasted_iota(jnp.int32, (1, cols), 1).astype(F32)
    identity = onehot(own, cols)
    first = (identity + onehot(index["east_west"], cols)).astype(BF16)
    second = (identity + onehot(index["north_south"], cols)).astype(BF16)
    gather_sum[...] = nn(first, second).astype(BF16)
    edge = send_rows.shape[0] // 2
    chosen = jnp.concatenate([onehot(index["send_up"], edge), onehot(index["send_down"], edge)], axis=0)
    send_rows[...] = nt(chosen.astype(BF16), first).astype(BF16)

    place = lax.broadcasted_iota(jnp.int32, (fields, rows), 1)
    field = lax.broadcasted_iota(jnp.int32, (fields, rows), 0)
    inside = (place >= field * levels) & (place < (field + 1) * levels)
    gains = exact(coupling[...], jnp.where(inside, 1.0, 0.0))
    for f in range(fields):
        spreadmix[:, f * levels : (f + 1) * levels] = mix[f]
    for g in range(fields):
        wide[g * levels : (g + 1) * levels, :] = spreadmix[...] * gains[g : g + 1, :]
    high, low = split(wide[...])
    whi[...] = high
    wlo[...] = low

    order = onehot(index["by_class"], cols).astype(BF16)
    xh, xl = split(state[...])
    begin = nt(xh, order) + nt(xl, order)
    tendency[...] = begin
    work[...] = begin
    bound = index["bound"]
    later = jnp.where(own >= half, bound, 0.0)
    most, some = jnp.max(bound).astype(jnp.int32), jnp.max(later).astype(jnp.int32)

    def step(width, k, carry):
        x = work[:, :width]
        high, low = split(x)
        y = nn(whi[...], high) + nn(whi[...], low) + nn(wlo[...], high)
        work[:, :width] = jnp.where(bound[:, :width] > k.astype(F32), x + PHYSICS_RATE * jnp.tanh(y), x)
        return carry

    lax.fori_loop(0, some, partial(step, cols), 0)
    lax.fori_loop(some, most, partial(step, half), 0)

    high, low = split(work[...] - tendency[...])
    change = nn(high, order) + nn(low, order)
    tendency[...] = change
    slots = jnp.broadcast_to(index["slot"], (EXTRA, cols))
    high, low = split(jnp.concatenate([state[...] + change, slots], axis=0))
    spot = index["by_slot"]
    pair = cols // (outgoing.shape[0] // per)
    if pair != per:
        whole = spot.astype(jnp.int32)
        spot = (lax.div(whole, pair) * per + lax.rem(whole, pair)).astype(F32)
    to_slot = onehot(spot, outgoing.shape[0]).astype(BF16)
    outgoing[...] = nt(to_slot, high) + nt(to_slot, low)


def move(current, tendency, metric, dhi, dlo, gather_sum, send_rows, levels):
    rows, cols = current.shape
    width = dhi.shape[0]
    parts = []
    for start in range(0, cols, width):
        x = current[:, start : start + width]
        high, low = split(x)
        slopes = nn(high, dhi) + nn(low, dhi) + nn(high, dlo)
        u, v = x[:levels], x[levels : 2 * levels]
        fields = rows // levels
        u, v = jnp.concatenate([u] * fields, axis=0), jnp.concatenate([v] * fields, axis=0)
        parts.append(u * slopes[:, :width] + v * slopes[:, width:])
    rate = -jnp.concatenate(parts, axis=1)
    moved = current + TIME_STEP * rate + tendency / SUBSTEPS
    weighted = jnp.concatenate([metric * moved, jnp.broadcast_to(metric, (EXTRA, cols))], axis=0)
    high, low = split(weighted)
    return nn(high, gather_sum) + nn(low, gather_sum), nt(send_rows, high) + nt(send_rows, low)


def settle(local, from_next, from_prev, table, rows):
    edge = from_next.shape[0]
    place_next = onehot(table[FROM_NEXT : FROM_NEXT + 1, :], edge)
    place_prev = onehot(table[FROM_PREV : FROM_PREV + 1, :], edge)
    place = jnp.concatenate([place_next, place_prev], axis=0).astype(BF16)
    high, low = split(jnp.concatenate([from_next, from_prev], axis=0))
    total = local + tn(high, place) + tn(low, place)
    return total[:rows] / total[rows : rows + 1]


def exchange_kernel(
    levels, per, state, tendency, dhi, dlo, gather_sum, send_rows, table, outgoing, out, physics,
    arrived, sent, received, near_send, near_recv, far_send, far_recv,
):
    rows, cols = out.shape
    edge = sent.shape[1] // 2
    elems, faces = lax.axis_size("elem"), lax.axis_size("face")
    devices = elems * faces
    myself = lax.axis_index("elem") * faces + lax.axis_index("face")

    def device(by):
        other = lax.rem(myself + by, devices)
        return other, (other // faces, lax.rem(other, faces))

    barrier = pltpu.get_barrier_semaphore()

    def greet(i, carry):
        pl.semaphore_signal(barrier, inc=1, device_id=device(i)[1], device_id_type=pl.DeviceIdType.MESH)
        return carry

    lax.fori_loop(1, devices, greet, 0)

    def near(step, way):
        return pltpu.make_async_remote_copy(
            src_ref=sent.at[step, pl.ds(way * edge, edge)],
            dst_ref=received.at[step, pl.ds((1 - way) * edge, edge)],
            send_sem=near_send.at[step, way],
            recv_sem=near_recv.at[step, way],
            device_id=device(1 if way == 0 else devices - 1)[1],
            device_id_type=pl.DeviceIdType.MESH,
        )

    stride = next(n for n in (13, 11, 7, 5, 3, 1) if math.gcd(n, devices) == 1)

    def far(i):
        other, where = device(lax.rem(i * stride, devices))
        return pltpu.make_async_remote_copy(
            src_ref=outgoing.at[pl.ds(pl.multiple_of(other * per, 8), per)],
            dst_ref=arrived.at[pl.ds(pl.multiple_of(myself * per, 8), per)],
            send_sem=far_send.at[i],
            recv_sem=far_recv.at[i],
            device_id=where,
            device_id_type=pl.DeviceIdType.MESH,
        )

    def start_far(i, carry):
        far(i).start()
        return carry

    def wait_far(i, carry):
        far(i).wait()
        return carry

    def advance(current):
        return move(
            current, tendency[...], table[WEIGHT : WEIGHT + 1, :], dhi[...], dlo[...], gather_sum[...], send_rows[...], levels
        )

    others = devices - 1
    cuts = [1, 1 + others * 7 // 31, 1 + others * 17 // 31, 1 + others * 27 // 31, devices]
    pl.semaphore_wait(barrier, others)
    lax.fori_loop(cuts[0], cuts[1], start_far, 0)
    local, edges = advance(state[...])
    sent[0] = edges
    near(0, 0).start()
    near(0, 1).start()
    mine = pl.ds(pl.multiple_of(myself * per, 8), per)
    arrived[mine, :] = outgoing[mine, :]
    for step in range(SUBSTEPS):
        near(step, 0).wait()
        near(step, 1).wait()
        lax.fori_loop(cuts[step + 1], cuts[step + 2], start_far, 0)
        current = settle(local, received[step, :edge], received[step, edge:], table[...], rows)
        if step < SUBSTEPS - 1:
            local, edges = advance(current)
            sent[step + 1] = edges
            near(step + 1, 0).start()
            near(step + 1, 1).start()
        else:
            out[...] = current
    lax.fori_loop(1, devices, wait_far, 0)
    slot = arrived[:, rows : rows + 1]
    places = lax.broadcasted_iota(jnp.int32, (arrived.shape[0], cols), 1).astype(F32)
    put = jnp.where(places == slot - (myself * cols).astype(F32), 1.0, 0.0).astype(BF16)
    high, low = split(arrived[:, :rows])
    physics[...] = tn(high, put) + tn(low, put)


def call(kernel, out_shape, scratch=(), inputs=1, **params):
    vmem = pl.BlockSpec(memory_space=pltpu.VMEM)
    return pl.pallas_call(
        kernel,
        out_shape=out_shape,
        in_specs=[vmem] * inputs,
        out_specs=jax.tree.map(lambda _: vmem, out_shape),
        scratch_shapes=list(scratch),
        compiler_params=pltpu.CompilerParams(vmem_limit_bytes=VMEM_LIMIT, **params),
    )


def per_device(state, metric, neighbours, cost_class, batch_slot, level_mix, field_coupling_matrix):
    fields, levels, cols = state.shape
    points, members = metric.shape
    rows = fields * levels
    edge = 4 * (members // ROWS_DEV)
    myself = lax.axis_index(AXES)
    devices = lax.axis_size(AXES)
    per = -(-(cols // devices) // 8) * 8
    slots = lax.dynamic_slice_in_dim(batch_slot, myself * members, members, axis=1)
    flat = state.reshape(rows, cols)
    dhi, dlo = (jnp.asarray(m) for m in derivative_operators(min(cols, 256)))

    shape = jax.ShapeDtypeStruct
    tendency, outgoing, gather_sum, send_rows, table = call(
        partial(physics_kernel, per),
        (
            shape((rows, cols), F32),
            shape((devices * per, rows + EXTRA), F32),
            shape((cols, cols), BF16),
            shape((2 * edge, cols), BF16),
            shape((TABLE_ROWS, cols), F32),
        ),
        (
            pltpu.VMEM((rows, rows), BF16),
            pltpu.VMEM((rows, rows), BF16),
            pltpu.VMEM((rows, rows), F32),
            pltpu.VMEM((rows, cols), F32),
            pltpu.VMEM((levels, rows), F32),
        ),
        inputs=7,
    )(flat, metric, neighbours, cost_class, slots, level_mix, field_coupling_matrix)
    out, physics = call(
        partial(exchange_kernel, levels, per),
        (shape((rows, cols), F32), shape((rows, cols), F32)),
        (
            pltpu.VMEM((devices * per, rows + EXTRA), F32),
            pltpu.VMEM((SUBSTEPS, 2 * edge, rows + EXTRA), F32),
            pltpu.VMEM((SUBSTEPS, 2 * edge, rows + EXTRA), F32),
            pltpu.SemaphoreType.DMA((SUBSTEPS, 2)),
            pltpu.SemaphoreType.DMA((SUBSTEPS, 2)),
            pltpu.SemaphoreType.DMA((devices,)),
            pltpu.SemaphoreType.DMA((devices,)),
        ),
        inputs=8,
        collective_id=0,
        has_side_effects=True,
    )(flat, tendency, dhi, dlo, gather_sum, send_rows, table, outgoing)
    return out.reshape(state.shape), physics.reshape(state.shape)


def solution(mesh):
    split_cols = P(None, AXES)
    return jax.shard_map(
        per_device,
        mesh=mesh,
        in_specs=(P(None, None, AXES), split_cols, split_cols, split_cols, P(), P(), P()),
        out_specs=(P(None, None, AXES), P(None, None, AXES)),
        check_vma=False,
    )
```

```python
from functools import partial

import jax
import jax.numpy as jnp
import numpy as np
from jax import lax
from jax.experimental import pallas as pl
from jax.experimental.pallas import tpu as pltpu
from jax.sharding import PartitionSpec as P

ROWS_DEV = 4
SUBSTEPS = 3
SWEEPS = 4
CLASSES = 4
PHYSICS_RATE = 0.1
TIME_STEP = 0.02
AXES = ("elem", "face")
EXTRA = 8
F32, BF16 = jnp.float32, jnp.bfloat16
VMEM_LIMIT = 56 * 1024 * 1024

FROM_NEXT, FROM_PREV, WEIGHT = range(3)
TABLE_ROWS = 8
FAR_AWAY = float(2**24)


def derivative_matrix():
    nodes = np.array([-1.0, -1.0 / np.sqrt(5.0), 1.0 / np.sqrt(5.0), 1.0])
    derivative = np.zeros((4, 4))
    for i in range(4):
        for j in range(4):
            if i == j:
                derivative[i, j] = sum(1.0 / (nodes[j] - nodes[m]) for m in range(4) if m != j)
            else:
                top = np.prod([nodes[i] - nodes[m] for m in range(4) if m not in (i, j)])
                derivative[i, j] = top / np.prod([nodes[j] - nodes[m] for m in range(4) if m != j])
    return derivative


def derivative_operators(width):
    derivative = derivative_matrix()
    blocks = np.eye(width // 16)
    across = np.kron(blocks, np.kron(np.eye(4), derivative)).T
    upward = np.kron(blocks, np.kron(derivative, np.eye(4))).T
    both = np.concatenate([across, upward], axis=1).astype(np.float32)
    high = both.astype(jnp.bfloat16)
    low = (both - high.astype(np.float32)).astype(jnp.bfloat16)
    return high, low


def split(values):
    high = values.astype(BF16)
    return high, (values - high.astype(F32)).astype(BF16)


def nn(a, b):
    return jnp.dot(a, b, preferred_element_type=F32)


def nt(a, b):
    return lax.dot_general(a, b, (((1,), (1,)), ((), ())), preferred_element_type=F32)


def tn(a, b):
    return lax.dot_general(a, b, (((0,), (0,)), ((), ())), preferred_element_type=F32)


def onehot(row, count):
    picks = lax.broadcasted_iota(jnp.int32, (count, row.shape[1]), 0).astype(F32)
    return jnp.where(picks == row, 1.0, 0.0).astype(F32)


def exact(a, b):
    return jnp.dot(a, b, precision=lax.Precision.HIGHEST, preferred_element_type=F32)


def index_rows(metric, neighbours, classes, slots):
    points, members = metric.shape
    cols = points * members
    base = ((lax.axis_index("elem") * lax.axis_size("face") + lax.axis_index("face")) * members).astype(F32)
    shift = points.bit_length() - 1
    own = lax.broadcasted_iota(jnp.int32, (1, cols), 1)
    element, point = (own >> shift).astype(F32), own & (points - 1)
    ix, iy = (point & 3).astype(F32), (point >> 2).astype(F32)
    leading = point == 0
    sequence = own.astype(F32)
    stacked = jnp.concatenate([metric, classes.astype(F32), slots.astype(F32)], axis=0)
    spread = onehot(element, members)
    rows = exact(stacked, spread)
    mine = lax.broadcasted_iota(jnp.int32, (points, cols), 0) == point
    weight, cost, slot = (
        jnp.sum(jnp.where(mine, rows[i * points : (i + 1) * points], 0.0), axis=0, keepdims=True) for i in range(3)
    )
    near = exact(neighbours.astype(F32), spread) - base
    east, west, north, south = (near[i : i + 1] for i in range(4))
    up = (north < 0.0) | (north >= members)
    down = (south < 0.0) | (south >= members)
    top, bottom = iy == 3.0, iy == 0.0

    keys = jnp.concatenate(
        [
            sequence - cost * cols,
            slot,
            jnp.where(up & leading, element, FAR_AWAY),
            jnp.where(down & leading, element, FAR_AWAY),
            jnp.where(up & leading, north, FAR_AWAY),
            jnp.where(down & leading, south, FAR_AWAY),
            sequence,
            sequence,
        ],
        axis=0,
    )
    turned = jnp.transpose(keys)

    def rank(i, values):
        return jnp.sum(jnp.where(turned[:, i : i + 1] < values, 1.0, 0.0), axis=0, keepdims=True)

    east_west = jnp.where(
        ix == 3.0, points * east + 4.0 * iy, jnp.where(ix == 0.0, points * west + 4.0 * iy + 3.0, -1.0)
    )
    north_south = jnp.where(
        top & ~up, points * north + ix, jnp.where(bottom & ~down, points * south + 12.0 + ix, -1.0)
    )
    send_up = jnp.where(top & up, 4.0 * rank(2, element) + ix, -1.0)
    send_down = jnp.where(bottom & down, 4.0 * rank(3, element) + ix, -1.0)
    from_next = jnp.where(top & up, 4.0 * rank(4, north) + ix, -1.0)
    from_prev = jnp.where(bottom & down, 4.0 * rank(5, south) + ix, -1.0)
    ordered = jnp.zeros((1, cols), F32)
    for q in range(1, CLASSES + 1):
        count = jnp.sum(jnp.where(cost >= q, 1.0, 0.0), axis=1, keepdims=True)
        ordered += jnp.where(sequence < count, 1.0, 0.0)
    return {
        "east_west": east_west,
        "north_south": north_south,
        "send_up": send_up,
        "send_down": send_down,
        "from_next": from_next,
        "from_prev": from_prev,
        "by_class": rank(0, keys[0:1]),
        "by_slot": rank(1, slot),
        "slot": slot,
        "weight": weight,
        "bound": ordered * SWEEPS,
    }


def physics_kernel(
    per, state, metric, neighbours, classes, slots, mix, coupling,
    tendency, outgoing, gather_sum, send_rows, table, whi, wlo, wide, work, spreadmix,
):
    rows, cols = state.shape
    fields, levels, _ = mix.shape
    half = cols // 2
    index = index_rows(metric[...], neighbours[...], classes[...], slots[...])
    blank = jnp.zeros((TABLE_ROWS - 3, cols), F32)
    table[...] = jnp.concatenate([index["from_next"], index["from_prev"], index["weight"], blank], axis=0)

    own = lax.broadcasted_iota(jnp.int32, (1, cols), 1).astype(F32)
    identity = onehot(own, cols)
    first = (identity + onehot(index["east_west"], cols)).astype(BF16)
    second = (identity + onehot(index["north_south"], cols)).astype(BF16)
    gather_sum[...] = nn(first, second).astype(BF16)
    edge = send_rows.shape[0] // 2
    chosen = jnp.concatenate([onehot(index["send_up"], edge), onehot(index["send_down"], edge)], axis=0)
    send_rows[...] = nt(chosen.astype(BF16), first).astype(BF16)

    place = lax.broadcasted_iota(jnp.int32, (fields, rows), 1)
    field = lax.broadcasted_iota(jnp.int32, (fields, rows), 0)
    inside = (place >= field * levels) & (place < (field + 1) * levels)
    gains = exact(coupling[...], jnp.where(inside, 1.0, 0.0))
    for f in range(fields):
        spreadmix[:, f * levels : (f + 1) * levels] = mix[f]
    for g in range(fields):
        wide[g * levels : (g + 1) * levels, :] = spreadmix[...] * gains[g : g + 1, :]
    high, low = split(wide[...])
    whi[...] = high
    wlo[...] = low

    order = onehot(index["by_class"], cols).astype(BF16)
    xh, xl = split(state[...])
    begin = nt(xh, order) + nt(xl, order)
    tendency[...] = begin
    work[...] = begin
    bound = index["bound"]
    later = jnp.where(own >= half, bound, 0.0)
    most, some = jnp.max(bound).astype(jnp.int32), jnp.max(later).astype(jnp.int32)

    def step(width, k, carry):
        x = work[:, :width]
        high, low = split(x)
        y = nn(whi[...], high) + nn(whi[...], low) + nn(wlo[...], high)
        work[:, :width] = jnp.where(bound[:, :width] > k.astype(F32), x + PHYSICS_RATE * jnp.tanh(y), x)
        return carry

    lax.fori_loop(0, some, partial(step, cols), 0)
    lax.fori_loop(some, most, partial(step, half), 0)

    high, low = split(work[...] - tendency[...])
    change = nn(high, order) + nn(low, order)
    tendency[...] = change
    slots = jnp.broadcast_to(index["slot"], (EXTRA, cols))
    high, low = split(jnp.concatenate([state[...] + change, slots], axis=0))
    spot = index["by_slot"]
    pair = cols // (outgoing.shape[0] // per)
    if pair != per:
        whole = spot.astype(jnp.int32)
        spot = (lax.div(whole, pair) * per + lax.rem(whole, pair)).astype(F32)
    to_slot = onehot(spot, outgoing.shape[0]).astype(BF16)
    outgoing[...] = nt(to_slot, high) + nt(to_slot, low)


def move(current, tendency, metric, dhi, dlo, gather_sum, send_rows, levels):
    rows, cols = current.shape
    width = dhi.shape[0]
    parts = []
    for start in range(0, cols, width):
        x = current[:, start : start + width]
        high, low = split(x)
        slopes = nn(high, dhi) + nn(low, dhi) + nn(high, dlo)
        u, v = x[:levels], x[levels : 2 * levels]
        fields = rows // levels
        u, v = jnp.concatenate([u] * fields, axis=0), jnp.concatenate([v] * fields, axis=0)
        parts.append(u * slopes[:, :width] + v * slopes[:, width:])
    rate = -jnp.concatenate(parts, axis=1)
    moved = current + TIME_STEP * rate + tendency / SUBSTEPS
    weighted = jnp.concatenate([metric * moved, jnp.broadcast_to(metric, (EXTRA, cols))], axis=0)
    high, low = split(weighted)
    return nn(high, gather_sum) + nn(low, gather_sum), nt(send_rows, high) + nt(send_rows, low)


def settle(local, from_next, from_prev, table, rows):
    edge = from_next.shape[0]
    place_next = onehot(table[FROM_NEXT : FROM_NEXT + 1, :], edge)
    place_prev = onehot(table[FROM_PREV : FROM_PREV + 1, :], edge)
    place = jnp.concatenate([place_next, place_prev], axis=0).astype(BF16)
    high, low = split(jnp.concatenate([from_next, from_prev], axis=0))
    total = local + tn(high, place) + tn(low, place)
    return total[:rows] / total[rows : rows + 1]


def exchange_kernel(
    levels, per, state, tendency, dhi, dlo, gather_sum, send_rows, table, outgoing, out, physics,
    arrived, sent, received, near_send, near_recv, far_send, far_recv,
):
    rows, cols = out.shape
    edge = sent.shape[1] // 2
    elems, faces = lax.axis_size("elem"), lax.axis_size("face")
    devices = elems * faces
    myself = lax.axis_index("elem") * faces + lax.axis_index("face")

    def device(by):
        other = lax.rem(myself + by, devices)
        return other, (other // faces, lax.rem(other, faces))

    barrier = pltpu.get_barrier_semaphore()

    def greet(i, carry):
        pl.semaphore_signal(barrier, inc=1, device_id=device(i)[1], device_id_type=pl.DeviceIdType.MESH)
        return carry

    lax.fori_loop(1, devices, greet, 0)

    def near(step, way):
        return pltpu.make_async_remote_copy(
            src_ref=sent.at[step, pl.ds(way * edge, edge)],
            dst_ref=received.at[step, pl.ds((1 - way) * edge, edge)],
            send_sem=near_send.at[step, way],
            recv_sem=near_recv.at[step, way],
            device_id=device(1 if way == 0 else devices - 1)[1],
            device_id_type=pl.DeviceIdType.MESH,
        )

    def far(i):
        other, where = device(i)
        return pltpu.make_async_remote_copy(
            src_ref=outgoing.at[pl.ds(pl.multiple_of(other * per, 8), per)],
            dst_ref=arrived.at[pl.ds(pl.multiple_of(myself * per, 8), per)],
            send_sem=far_send.at[i],
            recv_sem=far_recv.at[i],
            device_id=where,
            device_id_type=pl.DeviceIdType.MESH,
        )

    def start_far(i, carry):
        far(i).start()
        return carry

    def wait_far(i, carry):
        far(i).wait()
        return carry

    def advance(current):
        return move(
            current, tendency[...], table[WEIGHT : WEIGHT + 1, :], dhi[...], dlo[...], gather_sum[...], send_rows[...], levels
        )

    others = devices - 1
    cuts = [1, 1 + others * 6 // 31, 1 + others * 14 // 31, 1 + others * 22 // 31, devices]
    pl.semaphore_wait(barrier, others)
    lax.fori_loop(cuts[0], cuts[1], start_far, 0)
    local, edges = advance(state[...])
    sent[0] = edges
    near(0, 0).start()
    near(0, 1).start()
    mine = pl.ds(pl.multiple_of(myself * per, 8), per)
    arrived[mine, :] = outgoing[mine, :]
    for step in range(SUBSTEPS):
        near(step, 0).wait()
        near(step, 1).wait()
        lax.fori_loop(cuts[step + 1], cuts[step + 2], start_far, 0)
        current = settle(local, received[step, :edge], received[step, edge:], table[...], rows)
        if step < SUBSTEPS - 1:
            local, edges = advance(current)
            sent[step + 1] = edges
            near(step + 1, 0).start()
            near(step + 1, 1).start()
        else:
            out[...] = current
    lax.fori_loop(1, devices, wait_far, 0)
    slot = arrived[:, rows : rows + 1]
    places = lax.broadcasted_iota(jnp.int32, (arrived.shape[0], cols), 1).astype(F32)
    put = jnp.where(places == slot - (myself * cols).astype(F32), 1.0, 0.0).astype(BF16)
    high, low = split(arrived[:, :rows])
    physics[...] = tn(high, put) + tn(low, put)


def call(kernel, out_shape, scratch=(), inputs=1, **params):
    vmem = pl.BlockSpec(memory_space=pltpu.VMEM)
    return pl.pallas_call(
        kernel,
        out_shape=out_shape,
        in_specs=[vmem] * inputs,
        out_specs=jax.tree.map(lambda _: vmem, out_shape),
        scratch_shapes=list(scratch),
        compiler_params=pltpu.CompilerParams(vmem_limit_bytes=VMEM_LIMIT, **params),
    )


def per_device(state, metric, neighbours, cost_class, batch_slot, level_mix, field_coupling_matrix):
    fields, levels, cols = state.shape
    points, members = metric.shape
    rows = fields * levels
    edge = 4 * (members // ROWS_DEV)
    myself = lax.axis_index(AXES)
    devices = lax.axis_size(AXES)
    per = -(-(cols // devices) // 8) * 8
    slots = lax.dynamic_slice_in_dim(batch_slot, myself * members, members, axis=1)
    flat = state.reshape(rows, cols)
    dhi, dlo = (jnp.asarray(m) for m in derivative_operators(min(cols, 256)))

    shape = jax.ShapeDtypeStruct
    tendency, outgoing, gather_sum, send_rows, table = call(
        partial(physics_kernel, per),
        (
            shape((rows, cols), F32),
            shape((devices * per, rows + EXTRA), F32),
            shape((cols, cols), BF16),
            shape((2 * edge, cols), BF16),
            shape((TABLE_ROWS, cols), F32),
        ),
        (
            pltpu.VMEM((rows, rows), BF16),
            pltpu.VMEM((rows, rows), BF16),
            pltpu.VMEM((rows, rows), F32),
            pltpu.VMEM((rows, cols), F32),
            pltpu.VMEM((levels, rows), F32),
        ),
        inputs=7,
    )(flat, metric, neighbours, cost_class, slots, level_mix, field_coupling_matrix)
    out, physics = call(
        partial(exchange_kernel, levels, per),
        (shape((rows, cols), F32), shape((rows, cols), F32)),
        (
            pltpu.VMEM((devices * per, rows + EXTRA), F32),
            pltpu.VMEM((SUBSTEPS, 2 * edge, rows + EXTRA), F32),
            pltpu.VMEM((SUBSTEPS, 2 * edge, rows + EXTRA), F32),
            pltpu.SemaphoreType.DMA((SUBSTEPS, 2)),
            pltpu.SemaphoreType.DMA((SUBSTEPS, 2)),
            pltpu.SemaphoreType.DMA((devices,)),
            pltpu.SemaphoreType.DMA((devices,)),
        ),
        inputs=8,
        collective_id=0,
        has_side_effects=True,
    )(flat, tendency, dhi, dlo, gather_sum, send_rows, table, outgoing)
    return out.reshape(state.shape), physics.reshape(state.shape)


def solution(mesh):
    split_cols = P(None, AXES)
    return jax.shard_map(
        per_device,
        mesh=mesh,
        in_specs=(P(None, None, AXES), split_cols, split_cols, split_cols, P(), P(), P()),
        out_specs=(P(None, None, AXES), P(None, None, AXES)),
        check_vma=False,
    )
```
